32 devices in a mesh: vox: 8 (over y, x, core), frm: 4 (over z).
Axes of the slice: x: 2, y: 2, z: 4, core: 2. Of those that a mesh axis runs over, the one named last changes fastest.
Arguments:
- volume: bfloat16 [512, 32, 128], P('vox', 'frm'), parts along dimension 1, may hold values from 0.099609375 to 2
- measured: bfloat16 [512, 32, 128], P('vox', 'frm'), parts along dimension 1, may hold values from 0.19921875 to 3
- background: float32 [32], P('frm'), parts along dimension 0, may hold values from 0.05 to 0.5
- psf_tiles: bfloat16 [12, 128, 128], replicated, may hold values from 0 to 0.0025939941
- pair_sensor: int32 [8, 12, 64], P('vox'), may hold values from 0 to 63, as said below
- pair_voxel: int32 [8, 12, 64], P('vox'), may hold values from 0 to 511, as said below
- pair_count: int32 [8, 12], P('vox'), may hold values from 1 to 64, as said below
Outputs:
- updated: float32 [512, 32, 128], P('vox', 'frm'), parts along dimension 1
The draws below stay inside these ranges and needn't reach their ends.
There are 4 independent parts, one for each index of `frm`. The reference program is written for one: setup_inputs(seed, part) draws one part's arguments, and reference() takes and returns one part's arrays. A program takes and returns all parts, laid end to end along the dimension named above; an argument that names none is the same for every part. Nothing has to cross between parts.
Inputs may be any that keep to these rules, and one draw needn't show every extreme that they name: `pair_sensor`: the local index of a pair's sensor block among the 64 blocks of the list's own device; within one device's list for one offset all 64 slots name different sensor blocks. `pair_voxel`: a pair in device i's lists names a voxel block held by a device at most 3 positions from i along vox, inside the grid; within one device's list for one offset all 64 slots name different voxel blocks; the list of offset 0 names each of device i's own voxel blocks exactly once. `pair_count`: the live slots of a list are its first ones; every list of offset 0 is full, and for every offset some device's list is full.
All inputs are finite; a program needn't handle non-finite values.
Results may differ from the reference program's by a relative error of at most 0.0003.
Values may be sent and summed in bfloat16 or wider, within the bound.
A program may use at most 64 MiB of HBM per device.

```python
import math
import jax
import jax.numpy as jnp
from jax import lax

BLK_DEV = 64
FR = 8
NOFF = 12
REACH = 3
CAP = 64
VB = 512
N_VOX = 8


def draw_order(key):
    return jax.random.permutation(key, BLK_DEV)


def draw_pair_sensor(key, part):
    key = jax.random.fold_in(key, 13)
    orders = jax.vmap(draw_order)(jax.random.split(key, N_VOX * NOFF))
    return orders[:, :CAP].reshape(N_VOX, NOFF, CAP).astype(jnp.int32)


def draw_pair_voxel(key, part):
    key = jax.random.fold_in(key, 11)
    key_shift, key_order = jax.random.split(key, 2)
    device = jnp.arange(N_VOX, dtype=jnp.int32)[:, None, None]
    slot_index = jnp.arange(CAP, dtype=jnp.int32)[None, None, :]
    offset_index = jnp.arange(NOFF, dtype=jnp.int32)[None, :, None]
    shifts = jax.random.randint(key_shift, (N_VOX, NOFF, CAP), -REACH, REACH + 1)
    shifts = jnp.where((offset_index == 1) & (slot_index == 0), REACH, shifts)
    shifts = jnp.where((offset_index == 2) & (slot_index == 0), -REACH, shifts)
    shifts = jnp.where(offset_index == 0, 0, shifts)
    source = jnp.clip(device + shifts, 0, N_VOX - 1)
    orders = jax.vmap(draw_order)(jax.random.split(key_order, N_VOX * NOFF))
    local_block = orders[:, :CAP].reshape(N_VOX, NOFF, CAP)
    return (source * BLK_DEV + local_block).astype(jnp.int32)


def draw_pair_count(key, part):
    key = jax.random.fold_in(key, 12)
    key_load, key_levels, key_full = jax.random.split(key, 3)
    device_load = jax.random.randint(key_load, (N_VOX, 1), 1, 5)
    levels = jax.random.randint(key_levels, (N_VOX, NOFF), 1, 9)
    counts = jnp.clip(CAP * device_load * levels // 8, 1, CAP)
    full_device = jax.random.randint(key_full, (1, NOFF), 0, N_VOX)
    device = jnp.arange(N_VOX, dtype=jnp.int32)[:, None]
    counts = jnp.where(device == full_device, CAP, counts)
    counts = jnp.where(jnp.arange(NOFF, dtype=jnp.int32)[None, :] == 0, CAP, counts)
    return counts.astype(jnp.int32)


def shard_levels(stream_key, dims, pieces, least, top_value):
    level, own = 1.0, jax.random.fold_in(stream_key, 6)
    for dim, shards_of in pieces:
        draws = jnp.exp(jax.random.uniform(jax.random.fold_in(own, dim), (shards_of,), jnp.float32, least / len(pieces), top_value / len(pieces)))
        level = level * jnp.repeat(draws, dims[dim] // shards_of).reshape([-1 if axis == dim else 1 for axis in range(len(dims))])
    return level


def setup_inputs(seed: int = 0, part: int = 0) -> dict:
    key_list = jax.random.split(jax.random.key(seed), 8)
    own_keys = jax.random.split(jax.random.fold_in(key_list[7], part), 8)
    return {
        "volume": jnp.clip(0.099609375 + 1.9003906 * jax.random.uniform(own_keys[0], (VB, FR, 128), jnp.float32) ** shard_levels(own_keys[0], (VB, FR, 128), ((0, 8),), -0.2, 0.2), 0.099609375, 2.0).astype(jnp.bfloat16),
        "measured": jnp.clip(0.19921875 + 2.8007812 * jax.random.uniform(own_keys[1], (VB, FR, 128), jnp.float32) ** shard_levels(own_keys[1], (VB, FR, 128), ((0, 8),), -0.2, 0.2), 0.19921875, 3.0).astype(jnp.bfloat16),
        "background": jnp.clip(jnp.exp(jax.random.uniform(own_keys[2], (FR,), jnp.float32, math.log(0.05), math.log(0.5))), 0.05, 0.5),
        "psf_tiles": jnp.clip(jax.random.uniform(key_list[3], (NOFF, 128, 128), jnp.float32, 0.0, 0.0025939941), 0.0, 0.0025939941).astype(jnp.bfloat16),
        "pair_sensor": draw_pair_sensor(jax.random.fold_in(key_list[7], 71), part),
        "pair_voxel": draw_pair_voxel(jax.random.fold_in(key_list[7], 71), part),
        "pair_count": draw_pair_count(jax.random.fold_in(key_list[7], 71), part),
    }


def reference(volume, measured, background, psf_tiles, pair_sensor, pair_voxel, pair_count):
    blocks_all = volume.shape[0]
    slot_count = pair_sensor.shape[2]
    device = jnp.arange(N_VOX, dtype=jnp.int32)
    sensor_ids = device[:, None, None] * BLK_DEV + pair_sensor
    live_mask = jnp.arange(slot_count, dtype=jnp.int32)[None, None, :] < pair_count[:, :, None]
    sensor_put = jnp.where(live_mask, sensor_ids, blocks_all).astype(jnp.int32)
    voxel_put = jnp.where(live_mask, pair_voxel, blocks_all).astype(jnp.int32)

    def spread(source, take_all, put_all, transposed):
        frames = source.shape[1]

        def per_offset(totals, offset):
            psf_tile = psf_tiles[offset]
            take_ids = take_all[:, offset, :].reshape(-1)
            put_ids = put_all[:, offset, :].reshape(-1)
            gathered = jnp.take(source, take_ids, axis=0).reshape(-1, 128)
            if transposed:
                product = lax.dot_general(gathered, psf_tile, (((1,), (1,)), ((), ())), preferred_element_type=jnp.float32)
            else:
                product = jnp.dot(gathered, psf_tile, preferred_element_type=jnp.float32)
            totals = totals.at[put_ids].add(product.reshape(-1, frames, 128))
            return totals, None

        empty_sum = jnp.zeros((blocks_all + 1, frames, 128), jnp.float32)
        totals, unused = lax.scan(per_offset, empty_sum, jnp.arange(NOFF, dtype=jnp.int32))
        return totals[:blocks_all]

    projected = spread(volume, pair_voxel, sensor_put, False)
    ratio_image = (measured.astype(jnp.float32) / (projected + background.astype(jnp.float32)[None, :, None])).astype(jnp.bfloat16)
    extended = jnp.concatenate([ratio_image, jnp.ones((blocks_all, 1, 128), jnp.bfloat16)], axis=1)
    backproj = spread(extended, sensor_ids, voxel_put, True)
    return volume.astype(jnp.float32) * backproj[:, :FR] / backproj[:, FR:]
```

```python
import functools

import jax
import jax.numpy as jnp
from jax import lax
from jax.experimental import pallas as pl
from jax.experimental.pallas import tpu as pltpu
from jax.sharding import PartitionSpec as P

REACH = 3
PANELS = 2 * REACH + 2
FAR = -1000000.0
SHIFTS = (1, -1, 2, -2, 3, -3)


def update_kernel(
    count,
    chunks,
    volume_ref,
    measured_ref,
    background_ref,
    psf_ref,
    sensor_ref,
    voxel_ref,
    live_ref,
    out_ref,
    volume_win,
    ratio_win,
    voxel_win,
    volume_f32,
    measured_f32,
    place_fwd,
    place_bwd,
    psf_flat,
    psf_turned,
    ones_rows,
    norm,
    send_list,
    recv_list,
    send_vol,
    recv_vol,
    send_ratio,
    recv_ratio,
):
    me = lax.axis_index("vox")
    blocks, frames, width = volume_ref.shape
    offsets = psf_ref.shape[0]
    per = frames // chunks
    lanes = per * width
    f32, bf16 = jnp.float32, jnp.bfloat16

    def inside(shift):
        return (me + shift >= 0) & (me + shift < count)

    barrier = pltpu.get_barrier_semaphore()
    for shift in SHIFTS:

        @pl.when(inside(shift))
        def _():
            pl.semaphore_signal(
                barrier, inc=1, device_id={"vox": me + shift}, device_id_type=pl.DeviceIdType.MESH
            )

    volume_f32[...] = volume_ref[...].astype(f32).reshape(blocks * frames, width)
    for frame in range(frames):
        rows = volume_f32[pl.ds(frame, blocks, stride=frames), :]
        j, k = divmod(frame, per)
        volume_win[j, REACH, :, k * width : (k + 1) * width] = rows.astype(bf16)

    sensor_iota = lax.broadcasted_iota(jnp.int32, (blocks, blocks), 0)
    slot_iota = lax.broadcasted_iota(jnp.int32, (1, blocks), 1)
    lane_iota = lax.broadcasted_iota(jnp.int32, (blocks, 128), 1)
    by_sensor = []
    table = jnp.full((blocks, 128), FAR, f32)
    for o in range(offsets):
        live = slot_iota < live_ref[0, o]
        sensor_row = jnp.where(live, sensor_ref[0, o : o + 1, :], -1)
        voxel_row = voxel_ref[0, o : o + 1, :].astype(f32) - FAR
        column = jnp.sum(
            jnp.where(sensor_row == sensor_iota, voxel_row, 0.0), axis=1, keepdims=True
        ) + FAR
        by_sensor.append(column)
        table = jnp.where(lane_iota == o, column, table)
    voxel_win[REACH, :, :blocks] = table.T[:16, :]
    voxel_win[REACH, :, blocks:] = jnp.full((16, 128 - blocks), FAR, f32)

    pl.semaphore_wait(barrier, jnp.minimum(me, REACH) + jnp.minimum(count - 1 - me, REACH))

    def remote(buf, index, shift, send_sem, recv_sem):
        return pltpu.make_async_remote_copy(
            src_ref=buf.at[(*index, REACH)],
            dst_ref=buf.at[(*index, REACH - shift)],
            send_sem=send_sem,
            recv_sem=recv_sem,
            device_id={"vox": me + shift},
            device_id_type=pl.DeviceIdType.MESH,
        )

    def list_copy(i):
        shift = SHIFTS[i]
        return remote(voxel_win, (), shift, send_list.at[i], recv_list.at[i])

    def vol_copy(j, i):
        return remote(volume_win, (j,), SHIFTS[i], send_vol.at[j, i], recv_vol.at[j, i])

    def ratio_copy(j, i):
        return remote(ratio_win, (j,), SHIFTS[i], send_ratio.at[j, i], recv_ratio.at[j, i])

    def each(make, start):
        for i, shift in enumerate(SHIFTS):
            if start:

                @pl.when(inside(shift))
                def _():
                    make(i).start()

            else:

                @pl.when(inside(-shift))
                def _():
                    make(i).wait_recv()

    each(lambda i: vol_copy(0, i), True)
    each(list_copy, True)
    for j in range(1, chunks):
        each(functools.partial(vol_copy, j), True)

    for j in range(chunks):
        volume_win[j, PANELS - 1] = jnp.zeros((blocks, lanes), bf16)
        ratio_win[j, PANELS - 1] = jnp.zeros((blocks, lanes), bf16)
    for shift in SHIFTS:

        @pl.when(jnp.logical_not(inside(shift)))
        def _():
            for j in range(chunks):
                volume_win[j, REACH + shift] = jnp.zeros((blocks, lanes), bf16)
                ratio_win[j, REACH + shift] = jnp.zeros((blocks, lanes), bf16)
            voxel_win[REACH + shift] = jnp.full((16, 128), FAR, f32)

    base = ((me - REACH) * blocks).astype(f32)
    win_iota = lax.broadcasted_iota(jnp.int32, (1, PANELS * blocks), 1).astype(f32) + base
    for o in range(offsets):
        place_fwd[o * blocks : (o + 1) * blocks, :] = jnp.where(
            by_sensor[o] == win_iota, 1.0, 0.0
        ).astype(bf16)
        psf_flat[o * width : (o + 1) * width, :] = psf_ref[o]
        psf_turned[o * width : (o + 1) * width, :] = psf_ref[o].astype(f32).T.astype(bf16)
    measured_f32[...] = measured_ref[...].astype(f32).reshape(blocks * frames, width)

    each(list_copy, False)
    tables = jnp.concatenate(
        [voxel_win[d, :, :blocks] for d in range(PANELS - 1)]
        + [jnp.full((16, blocks), FAR, f32)],
        axis=1,
    )
    voxel_iota = lax.broadcasted_iota(jnp.int32, (blocks, 1), 0).astype(f32) + (
        me * blocks
    ).astype(f32)
    for o in range(offsets):
        hits = jnp.where(tables[o : o + 1, :] == voxel_iota, 1.0, 0.0)
        place_bwd[o * blocks : (o + 1) * blocks, :] = hits.astype(bf16)
        pairs = jnp.sum(hits, axis=1, keepdims=True)
        ones_rows[:, o * width : (o + 1) * width] = jnp.broadcast_to(pairs, (blocks, width)).astype(
            bf16
        )
    norm[...] = jnp.dot(ones_rows[...], psf_turned[...], preferred_element_type=f32)

    def joined(placed):
        return jnp.concatenate(
            [
                jnp.concatenate(
                    [
                        placed[o * blocks : (o + 1) * blocks, k * width : (k + 1) * width]
                        for o in range(offsets)
                    ],
                    axis=1,
                )
                for k in range(per)
            ],
            axis=0,
        )

    for j in range(chunks):
        each(functools.partial(vol_copy, j), False)
        window = volume_win[j].reshape(PANELS * blocks, lanes)
        placed = jnp.dot(place_fwd[...], window, preferred_element_type=f32).astype(bf16)
        projected = jnp.dot(joined(placed), psf_flat[...], preferred_element_type=f32)
        for k in range(per):
            frame = j * per + k
            recorded = measured_f32[pl.ds(frame, blocks, stride=frames), :]
            ratio = recorded / (projected[k * blocks : (k + 1) * blocks] + background_ref[0, frame])
            ratio_win[j, REACH, :, k * width : (k + 1) * width] = ratio.astype(bf16)
        each(functools.partial(ratio_copy, j), True)

    for j in range(chunks):
        each(functools.partial(ratio_copy, j), False)
        window = ratio_win[j].reshape(PANELS * blocks, lanes)
        summed = jnp.dot(place_bwd[...], window, preferred_element_type=f32)
        high = summed.astype(bf16)
        low = (summed - high.astype(f32)).astype(bf16)
        back = jnp.dot(joined(high), psf_turned[...], preferred_element_type=f32)
        back = back + jnp.dot(joined(low), psf_turned[...], preferred_element_type=f32)
        for k in range(per):
            frame = j * per + k
            current = volume_f32[pl.ds(frame, blocks, stride=frames), :]
            out_ref[pl.ds(frame, blocks, stride=frames), :] = (
                current * back[k * blocks : (k + 1) * blocks] / norm[...]
            )

    for i, shift in enumerate(SHIFTS):

        @pl.when(inside(shift))
        def _():
            list_copy(i).wait_send()
            for j in range(chunks):
                vol_copy(j, i).wait_send()
                ratio_copy(j, i).wait_send()


def local(count, volume, measured, background, psf_tiles, pair_sensor, pair_voxel, pair_count):
    blocks, frames, width = volume.shape
    offsets = psf_tiles.shape[0]
    chunks = 4
    lanes = frames // chunks * width
    vmem = pl.BlockSpec(memory_space=pltpu.VMEM)
    smem = pl.BlockSpec(memory_space=pltpu.SMEM)
    links = len(SHIFTS)
    dma = pltpu.SemaphoreType.DMA
    updated = pl.pallas_call(
        functools.partial(update_kernel, count, chunks),
        out_shape=jax.ShapeDtypeStruct((blocks * frames, width), jnp.float32),
        in_specs=[vmem, vmem, smem, vmem, vmem, vmem, smem],
        out_specs=vmem,
        scratch_shapes=[
            pltpu.VMEM((chunks, PANELS, blocks, lanes), jnp.bfloat16),
            pltpu.VMEM((chunks, PANELS, blocks, lanes), jnp.bfloat16),
            pltpu.VMEM((PANELS - 1, 16, 128), jnp.float32),
            pltpu.VMEM((blocks * frames, width), jnp.float32),
            pltpu.VMEM((blocks * frames, width), jnp.float32),
            pltpu.VMEM((offsets * blocks, PANELS * blocks), jnp.bfloat16),
            pltpu.VMEM((offsets * blocks, PANELS * blocks), jnp.bfloat16),
            pltpu.VMEM((offsets * width, width), jnp.bfloat16),
            pltpu.VMEM((offsets * width, width), jnp.bfloat16),
            pltpu.VMEM((blocks, offsets * width), jnp.bfloat16),
            pltpu.VMEM((blocks, width), jnp.float32),
            dma((links,)),
            dma((links,)),
            dma((chunks, links)),
            dma((chunks, links)),
            dma((chunks, links)),
            dma((chunks, links)),
        ],
        compiler_params=pltpu.CompilerParams(
            collective_id=0, has_side_effects=True, vmem_limit_bytes=40 * 1024 * 1024
        ),
    )(
        volume,
        measured,
        background.reshape(1, frames),
        psf_tiles,
        pair_sensor,
        pair_voxel,
        pair_count,
    )
    return updated.reshape(blocks, frames, width)


def solution(mesh):
    return jax.shard_map(
        functools.partial(local, mesh.shape["vox"]),
        mesh=mesh,
        in_specs=(
            P("vox", "frm", None),
            P("vox", "frm", None),
            P("frm"),
            P(),
            P("vox", None, None),
            P("vox", None, None),
            P("vox", None),
        ),
        out_specs=P("vox", "frm", None),
        check_vma=False,
    )
```

```python
import functools

import jax
import jax.numpy as jnp
from jax import lax
from jax.experimental import pallas as pl
from jax.experimental.pallas import tpu as pltpu
from jax.sharding import PartitionSpec as P

REACH = 3
PANELS = 2 * REACH + 2
FAR = -1000000.0
SHIFTS = (1, -1, 2, -2, 3, -3)
MESH = pl.DeviceIdType.MESH
OUT_KINDS = 7


def update_kernel(
    count,
    chunks,
    volume_hbm,
    measured_hbm,
    background_ref,
    psf_hbm,
    sensor_hbm,
    voxel_hbm,
    live_ref,
    out_ref,
    volume_ref,
    measured_ref,
    psf_ref,
    sensor_ref,
    voxel_ref,
    volume_win,
    ratio_win,
    voxel_win,
    volume_f32,
    measured_f32,
    place_fwd,
    place_bwd,
    psf_turned,
    ones_rows,
    norm,
    load_sem,
    send_list,
    recv_list,
    send_vol,
    recv_vol,
    send_ratio,
    recv_ratio,
):
    me = lax.axis_index("vox")
    core = lax.rem(me, 2)
    sibling = me + 1 - 2 * core
    blocks, frames, width = volume_ref.shape
    offsets = psf_ref.shape[0] // width
    per = frames // chunks
    lanes = per * width
    f32, bf16 = jnp.float32, jnp.bfloat16
    square = count == 8

    def inside(shift):
        return (me + shift >= 0) & (me + shift < count)

    loads = [
        pltpu.make_async_copy(source, target, load_sem.at[i])
        for i, (source, target) in enumerate(
            (
                (volume_hbm, volume_ref),
                (sensor_hbm, sensor_ref),
                (voxel_hbm, voxel_ref),
                (measured_hbm, measured_ref),
                (psf_hbm, psf_ref),
            )
        )
    ]
    for load in loads:
        load.start()

    barrier = pltpu.get_barrier_semaphore()
    for shift in SHIFTS:

        @pl.when(inside(shift))
        def _():
            pl.semaphore_signal(barrier, inc=1, device_id={"vox": me + shift}, device_id_type=MESH)

    peers = jnp.minimum(me, REACH) + jnp.minimum(count - 1 - me, REACH)
    if square:
        at_corner = (me == 0) | (me == 3) | (me == 4) | (me == 7)
        across = lax.rem(me + 4, 8)
        peers = peers + jnp.where(at_corner, 1, 0)

        @pl.when(at_corner)
        def _():
            pl.semaphore_signal(barrier, inc=1, device_id={"vox": across}, device_id_type=MESH)

    loads[0].wait()
    volume_f32[...] = volume_ref[...].astype(f32).reshape(blocks * frames, width)
    for frame in range(frames):
        rows = volume_f32[pl.ds(frame, blocks, stride=frames), :]
        j, k = divmod(frame, per)
        volume_win[j, REACH, :, k * width : (k + 1) * width] = rows.astype(bf16)

    pl.semaphore_wait(barrier, peers)

    class Panels:
        def __init__(self, win, send_sem, recv_sem):
            self.win, self.send_sem, self.recv_sem = win, send_sem, recv_sem

        def copy(self, j, kind, held, target):
            place = REACH + (me + held) - target
            return pltpu.make_async_remote_copy(
                src_ref=self.win.at[j, REACH + held],
                dst_ref=self.win.at[j, place],
                send_sem=self.send_sem.at[j, kind],
                recv_sem=self.recv_sem.at[j, place],
                device_id={"vox": target},
                device_id_type=MESH,
            )

        def wait_panel(self, j, place):
            pltpu.make_async_remote_copy(
                src_ref=self.win.at[j, REACH],
                dst_ref=self.win.at[j, REACH + place],
                send_sem=self.send_sem.at[j, 0],
                recv_sem=self.recv_sem.at[j, REACH + place],
                device_id={"vox": me},
                device_id_type=MESH,
            ).wait_recv()

        def own(self):
            far = me + 6 * core - 3
            direct_up, direct_down = inside(2), inside(-2)
            if square:
                direct_up = direct_up & (me != 2) & (me != 3)
                direct_down = direct_down & (me != 4) & (me != 5)
            return (
                (0, 0, far, (far >= 0) & (far < count)),
                (1, 0, me + 2, direct_up),
                (2, 0, me - 2, direct_down),
                (3, 0, sibling, me >= 0),
            )

        def passed(self):
            return ((4, 2, sibling, inside(2)), (5, -2, sibling, inside(-2)))

        def relays(self):
            if not square:
                return ()
            return (
                (6, 2, me + 4, me == 0),
                (6, -2, me - 4, me == 7),
                (6, 3, me + 1, me == 1),
                (6, -3, me - 1, me == 6),
            )

        def send_own(self, j):
            for kind, held, target, use in self.own():

                @pl.when(use)
                def _():
                    self.copy(j, kind, held, target).start()

        def pass_on(self, j):
            for shift in (2, -2):

                @pl.when(inside(shift))
                def _():
                    self.wait_panel(j, shift)

            far = 6 * core - 3

            @pl.when((me + far >= 0) & (me + far < count))
            def _():
                self.wait_panel(j, far)

            for kind, held, target, use in (*self.relays(), *self.passed()):

                @pl.when(use)
                def _():
                    self.copy(j, kind, held, target).start()

        def wait_rest(self, j):
            self.wait_panel(j, 1 - 2 * core)
            for shift in (2, -2):
                place = 1 - 2 * core + shift

                @pl.when((me + place >= 0) & (me + place < count))
                def _():
                    self.wait_panel(j, place)

        def wait_sent(self, j):
            for kind, held, target, use in (*self.own(), *self.relays(), *self.passed()):

                @pl.when(use)
                def _():
                    self.copy(j, kind, held, target).wait_send()

    volumes = Panels(volume_win, send_vol, recv_vol)
    ratios = Panels(ratio_win, send_ratio, recv_ratio)

    def list_copy(i):
        shift = SHIFTS[i]
        return pltpu.make_async_remote_copy(
            src_ref=voxel_win.at[REACH],
            dst_ref=voxel_win.at[REACH - shift],
            send_sem=send_list.at[i],
            recv_sem=recv_list.at[i],
            device_id={"vox": me + shift},
            device_id_type=MESH,
        )

    for j in range(chunks):
        volumes.send_own(j)

    loads[1].wait()
    loads[2].wait()
    sensor_iota = lax.broadcasted_iota(jnp.int32, (blocks, blocks), 0)
    slot_iota = lax.broadcasted_iota(jnp.int32, (1, blocks), 1)
    lane_iota = lax.broadcasted_iota(jnp.int32, (blocks, 128), 1)
    by_sensor = []
    table = jnp.full((blocks, 128), FAR, f32)
    for o in range(offsets):
        live = slot_iota < live_ref[0, o]
        sensor_row = jnp.where(live, sensor_ref[o], -1)
        voxel_row = voxel_ref[o].astype(f32) - FAR
        column = jnp.sum(
            jnp.where(sensor_row == sensor_iota, voxel_row, 0.0), axis=1, keepdims=True
        ) + FAR
        by_sensor.append(column)
        table = jnp.where(lane_iota == o, column, table)
    voxel_win[REACH, :, :blocks] = table.T[:16, :]
    voxel_win[REACH, :, blocks:] = jnp.full((16, 128 - blocks), FAR, f32)

    for i, shift in enumerate(SHIFTS):

        @pl.when(inside(shift))
        def _():
            list_copy(i).start()

    for j in range(chunks):
        volume_win[j, PANELS - 1] = jnp.zeros((blocks, lanes), bf16)
        ratio_win[j, PANELS - 1] = jnp.zeros((blocks, lanes), bf16)
    for shift in SHIFTS:

        @pl.when(jnp.logical_not(inside(shift)))
        def _():
            for j in range(chunks):
                volume_win[j, REACH + shift] = jnp.zeros((blocks, lanes), bf16)
                ratio_win[j, REACH + shift] = jnp.zeros((blocks, lanes), bf16)
            voxel_win[REACH + shift] = jnp.full((16, 128), FAR, f32)

    volumes.pass_on(0)

    base = ((me - REACH) * blocks).astype(f32)
    win_iota = lax.broadcasted_iota(jnp.int32, (1, PANELS * blocks), 1).astype(f32) + base
    for o in range(offsets):
        place_fwd[o * blocks : (o + 1) * blocks, :] = jnp.where(
            by_sensor[o] == win_iota, 1.0, 0.0
        ).astype(bf16)
    volumes.pass_on(1)

    loads[3].wait()
    measured_f32[...] = measured_ref[...].astype(f32).reshape(blocks * frames, width)
    loads[4].wait()

    def joined(placed):
        return jnp.concatenate(
            [
                jnp.concatenate(
                    [
                        placed[o * blocks : (o + 1) * blocks, k * width : (k + 1) * width]
                        for o in range(offsets)
                    ],
                    axis=1,
                )
                for k in range(per)
            ],
            axis=0,
        )

    def forward(j):
        volumes.wait_rest(j)
        window = volume_win[j].reshape(PANELS * blocks, lanes)
        placed = jnp.dot(place_fwd[...], window, preferred_element_type=f32).astype(bf16)
        projected = jnp.dot(joined(placed), psf_ref[...], preferred_element_type=f32)
        for k in range(per):
            frame = j * per + k
            recorded = measured_f32[pl.ds(frame, blocks, stride=frames), :]
            ratio = recorded / (projected[k * blocks : (k + 1) * blocks] + background_ref[0, frame])
            ratio_win[j, REACH, :, k * width : (k + 1) * width] = ratio.astype(bf16)
        ratios.send_own(j)

    def backward(j):
        ratios.wait_rest(j)
        window = ratio_win[j].reshape(PANELS * blocks, lanes)
        summed = jnp.dot(place_bwd[...], window, preferred_element_type=f32)
        high = summed.astype(bf16)
        low = (summed - high.astype(f32)).astype(bf16)
        back = jnp.dot(joined(high), psf_turned[...], preferred_element_type=f32)
        back = back + jnp.dot(joined(low), psf_turned[...], preferred_element_type=f32)
        for k in range(per):
            frame = j * per + k
            current = volume_f32[pl.ds(frame, blocks, stride=frames), :]
            out_ref[pl.ds(frame, blocks, stride=frames), :] = (
                current * back[k * blocks : (k + 1) * blocks] / norm[...]
            )

    forward(0)
    volumes.pass_on(2)
    forward(1)
    volumes.pass_on(3)
    ratios.pass_on(0)
    forward(2)
    ratios.pass_on(1)
    forward(3)
    ratios.pass_on(2)

    for i, shift in enumerate(SHIFTS):

        @pl.when(inside(-shift))
        def _():
            list_copy(i).wait_recv()

    for o in range(offsets):
        tile = slice(o * width, (o + 1) * width)
        psf_turned[tile, :] = psf_ref[tile, :].astype(f32).T.astype(bf16)
    tables = jnp.concatenate(
        [voxel_win[d, :, :blocks] for d in range(PANELS - 1)]
        + [jnp.full((16, blocks), FAR, f32)],
        axis=1,
    )
    voxel_iota = lax.broadcasted_iota(jnp.int32, (blocks, 1), 0).astype(f32) + (
        me * blocks
    ).astype(f32)
    for o in range(offsets):
        hits = jnp.where(tables[o : o + 1, :] == voxel_iota, 1.0, 0.0)
        place_bwd[o * blocks : (o + 1) * blocks, :] = hits.astype(bf16)
        pairs = jnp.sum(hits, axis=1, keepdims=True)
        ones_rows[:, o * width : (o + 1) * width] = jnp.broadcast_to(pairs, (blocks, width)).astype(
            bf16
        )
    norm[...] = jnp.dot(ones_rows[...], psf_turned[...], preferred_element_type=f32)

    ratios.pass_on(3)
    for j in range(chunks):
        backward(j)

    for i, shift in enumerate(SHIFTS):

        @pl.when(inside(shift))
        def _():
            list_copy(i).wait_send()

    for j in range(chunks):
        volumes.wait_sent(j)
        ratios.wait_sent(j)


def local(count, volume, measured, background, psf_tiles, pair_sensor, pair_voxel, pair_count):
    blocks, frames, width = volume.shape
    offsets = psf_tiles.shape[0]
    chunks = 4
    lanes = frames // chunks * width
    smem = pl.BlockSpec(memory_space=pltpu.SMEM)
    anywhere = pl.BlockSpec(memory_space=pl.ANY)
    links = len(SHIFTS)
    f32, bf16, dma = jnp.float32, jnp.bfloat16, pltpu.SemaphoreType.DMA
    updated = pl.pallas_call(
        functools.partial(update_kernel, count, chunks),
        out_shape=jax.ShapeDtypeStruct((blocks * frames, width), f32),
        in_specs=[anywhere, anywhere, smem, anywhere, anywhere, anywhere, smem],
        out_specs=pl.BlockSpec(memory_space=pltpu.VMEM),
        scratch_shapes=[
            pltpu.VMEM(volume.shape, bf16),
            pltpu.VMEM(measured.shape, bf16),
            pltpu.VMEM((offsets * width, width), bf16),
            pltpu.VMEM((offsets, 1, blocks), jnp.int32),
            pltpu.VMEM((offsets, 1, blocks), jnp.int32),
            pltpu.VMEM((chunks, PANELS, blocks, lanes), bf16),
            pltpu.VMEM((chunks, PANELS, blocks, lanes), bf16),
            pltpu.VMEM((PANELS - 1, 16, 128), f32),
            pltpu.VMEM((blocks * frames, width), f32),
            pltpu.VMEM((blocks * frames, width), f32),
            pltpu.VMEM((offsets * blocks, PANELS * blocks), bf16),
            pltpu.VMEM((offsets * blocks, PANELS * blocks), bf16),
            pltpu.VMEM((offsets * width, width), bf16),
            pltpu.VMEM((blocks, offsets * width), bf16),
            pltpu.VMEM((blocks, width), f32),
            dma((5,)),
            dma((links,)),
            dma((links,)),
            dma((chunks, OUT_KINDS)),
            dma((chunks, PANELS - 1)),
            dma((chunks, OUT_KINDS)),
            dma((chunks, PANELS - 1)),
        ],
        compiler_params=pltpu.CompilerParams(
            collective_id=0, has_side_effects=True, vmem_limit_bytes=56 * 1024 * 1024
        ),
    )(
        volume,
        measured,
        background.reshape(1, frames),
        psf_tiles.reshape(offsets * width, width),
        pair_sensor.reshape(offsets, 1, blocks),
        pair_voxel.reshape(offsets, 1, blocks),
        pair_count,
    )
    return updated.reshape(blocks, frames, width)


def solution(mesh):
    return jax.shard_map(
        functools.partial(local, mesh.shape["vox"]),
        mesh=mesh,
        in_specs=(
            P("vox", "frm", None),
            P("vox", "frm", None),
            P("frm"),
            P(),
            P("vox", None, None),
            P("vox", None, None),
            P("vox", None),
        ),
        out_specs=P("vox", "frm", None),
        check_vma=False,
    )
```

```python
import functools

import jax
import jax.numpy as jnp
from jax import lax
from jax.experimental import pallas as pl
from jax.experimental.pallas import tpu as pltpu
from jax.sharding import PartitionSpec as P

REACH = 3
PANELS = 2 * REACH + 2
FAR = -1000000.0
SHIFTS = (1, -1, 2, -2, 3, -3)
MESH = pl.DeviceIdType.MESH
OUT_KINDS = 6


def update_kernel(
    count,
    chunks,
    volume_hbm,
    measured_hbm,
    background_ref,
    psf_hbm,
    sensor_hbm,
    voxel_hbm,
    live_ref,
    out_ref,
    volume_ref,
    measured_ref,
    psf_ref,
    sensor_ref,
    voxel_ref,
    volume_win,
    ratio_win,
    voxel_win,
    volume_f32,
    measured_f32,
    place_fwd,
    place_bwd,
    psf_turned,
    ones_rows,
    norm,
    load_sem,
    send_list,
    recv_list,
    send_vol,
    recv_vol,
    send_ratio,
    recv_ratio,
):
    me = lax.axis_index("vox")
    core = lax.rem(me, 2)
    sibling = me + 1 - 2 * core
    blocks, frames, width = volume_ref.shape
    offsets = psf_ref.shape[0] // width
    per = frames // chunks
    lanes = per * width
    f32, bf16 = jnp.float32, jnp.bfloat16

    def inside(shift):
        return (me + shift >= 0) & (me + shift < count)

    loads = [
        pltpu.make_async_copy(source, target, load_sem.at[i])
        for i, (source, target) in enumerate(
            (
                (volume_hbm, volume_ref),
                (sensor_hbm, sensor_ref),
                (voxel_hbm, voxel_ref),
                (measured_hbm, measured_ref),
                (psf_hbm, psf_ref),
            )
        )
    ]
    for load in loads:
        load.start()

    barrier = pltpu.get_barrier_semaphore()
    for shift in SHIFTS:

        @pl.when(inside(shift))
        def _():
            pl.semaphore_signal(barrier, inc=1, device_id={"vox": me + shift}, device_id_type=MESH)

    peers = jnp.minimum(me, REACH) + jnp.minimum(count - 1 - me, REACH)

    loads[0].wait()
    volume_f32[...] = volume_ref[...].astype(f32).reshape(blocks * frames, width)
    for frame in range(frames):
        rows = volume_f32[pl.ds(frame, blocks, stride=frames), :]
        j, k = divmod(frame, per)
        volume_win[j, REACH, :, k * width : (k + 1) * width] = rows.astype(bf16)

    pl.semaphore_wait(barrier, peers)

    class Panels:
        def __init__(self, win, send_sem, recv_sem):
            self.win, self.send_sem, self.recv_sem = win, send_sem, recv_sem

        def copy(self, j, kind, held, target):
            place = REACH + (me + held) - target
            return pltpu.make_async_remote_copy(
                src_ref=self.win.at[j, REACH + held],
                dst_ref=self.win.at[j, place],
                send_sem=self.send_sem.at[j, kind],
                recv_sem=self.recv_sem.at[j, place],
                device_id={"vox": target},
                device_id_type=MESH,
            )

        def wait_panel(self, j, place):
            pltpu.make_async_remote_copy(
                src_ref=self.win.at[j, REACH],
                dst_ref=self.win.at[j, REACH + place],
                send_sem=self.send_sem.at[j, 0],
                recv_sem=self.recv_sem.at[j, REACH + place],
                device_id={"vox": me},
                device_id_type=MESH,
            ).wait_recv()

        def own(self):
            far = me + 6 * core - 3
            direct_up, direct_down = inside(2), inside(-2)
            return (
                (0, 0, far, (far >= 0) & (far < count)),
                (1, 0, me + 2, direct_up),
                (2, 0, me - 2, direct_down),
                (3, 0, sibling, me >= 0),
            )

        def passed(self):
            return ((4, 2, sibling, inside(2)), (5, -2, sibling, inside(-2)))

        def send_own(self, j):
            for kind, held, target, use in self.own():

                @pl.when(use)
                def _():
                    self.copy(j, kind, held, target).start()

        def pass_on(self, j):
            for shift in (2, -2):

                @pl.when(inside(shift))
                def _():
                    self.wait_panel(j, shift)

            for kind, held, target, use in self.passed():

                @pl.when(use)
                def _():
                    self.copy(j, kind, held, target).start()

        def wait_rest(self, j):
            self.wait_panel(j, 1 - 2 * core)
            far = 6 * core - 3

            @pl.when((me + far >= 0) & (me + far < count))
            def _():
                self.wait_panel(j, far)

            for shift in (2, -2):
                place = 1 - 2 * core + shift

                @pl.when((me + place >= 0) & (me + place < count))
                def _():
                    self.wait_panel(j, place)

        def wait_sent(self, j):
            for kind, held, target, use in (*self.own(), *self.passed()):

                @pl.when(use)
                def _():
                    self.copy(j, kind, held, target).wait_send()

    volumes = Panels(volume_win, send_vol, recv_vol)
    ratios = Panels(ratio_win, send_ratio, recv_ratio)

    def list_copy(i):
        shift = SHIFTS[i]
        return pltpu.make_async_remote_copy(
            src_ref=voxel_win.at[REACH],
            dst_ref=voxel_win.at[REACH - shift],
            send_sem=send_list.at[i],
            recv_sem=recv_list.at[i],
            device_id={"vox": me + shift},
            device_id_type=MESH,
        )

    volumes.send_own(0)

    loads[1].wait()
    loads[2].wait()
    sensor_iota = lax.broadcasted_iota(jnp.int32, (blocks, blocks), 0)
    slot_iota = lax.broadcasted_iota(jnp.int32, (1, blocks), 1)
    lane_iota = lax.broadcasted_iota(jnp.int32, (blocks, 128), 1)
    by_sensor = []
    table = jnp.full((blocks, 128), FAR, f32)
    for o in range(offsets):
        live = slot_iota < live_ref[0, o]
        sensor_row = jnp.where(live, sensor_ref[o], -1)
        voxel_row = voxel_ref[o].astype(f32) - FAR
        column = jnp.sum(
            jnp.where(sensor_row == sensor_iota, voxel_row, 0.0), axis=1, keepdims=True
        ) + FAR
        by_sensor.append(column)
        table = jnp.where(lane_iota == o, column, table)
    voxel_win[REACH, :, :blocks] = table.T[:16, :]
    voxel_win[REACH, :, blocks:] = jnp.full((16, 128 - blocks), FAR, f32)

    for i, shift in enumerate(SHIFTS):

        @pl.when(inside(shift))
        def _():
            list_copy(i).start()

    for j in range(1, chunks):
        volumes.send_own(j)

    for j in range(chunks):
        volume_win[j, PANELS - 1] = jnp.zeros((blocks, lanes), bf16)
        ratio_win[j, PANELS - 1] = jnp.zeros((blocks, lanes), bf16)
    for shift in SHIFTS:

        @pl.when(jnp.logical_not(inside(shift)))
        def _():
            for j in range(chunks):
                volume_win[j, REACH + shift] = jnp.zeros((blocks, lanes), bf16)
                ratio_win[j, REACH + shift] = jnp.zeros((blocks, lanes), bf16)
            voxel_win[REACH + shift] = jnp.full((16, 128), FAR, f32)

    def joined(placed):
        return jnp.concatenate(
            [
                jnp.concatenate(
                    [
                        placed[o * blocks : (o + 1) * blocks, k * width : (k + 1) * width]
                        for o in range(offsets)
                    ],
                    axis=1,
                )
                for k in range(per)
            ],
            axis=0,
        )

    def forward(j):
        volumes.wait_rest(j)
        window = volume_win[j].reshape(PANELS * blocks, lanes)
        placed = jnp.dot(place_fwd[...], window, preferred_element_type=f32).astype(bf16)
        projected = jnp.dot(joined(placed), psf_ref[...], preferred_element_type=f32)
        for k in range(per):
            frame = j * per + k
            recorded = measured_f32[pl.ds(frame, blocks, stride=frames), :]
            ratio = recorded / (projected[k * blocks : (k + 1) * blocks] + background_ref[0, frame])
            ratio_win[j, REACH, :, k * width : (k + 1) * width] = ratio.astype(bf16)
        ratios.send_own(j)

    def backward(j):
        ratios.wait_rest(j)
        window = ratio_win[j].reshape(PANELS * blocks, lanes)
        summed = jnp.dot(place_bwd[...], window, preferred_element_type=f32)
        high = summed.astype(bf16)
        low = (summed - high.astype(f32)).astype(bf16)
        back = jnp.dot(joined(high), psf_turned[...], preferred_element_type=f32)
        back = back + jnp.dot(joined(low), psf_turned[...], preferred_element_type=f32)
        for k in range(per):
            frame = j * per + k
            current = volume_f32[pl.ds(frame, blocks, stride=frames), :]
            out_ref[pl.ds(frame, blocks, stride=frames), :] = (
                current * back[k * blocks : (k + 1) * blocks] / norm[...]
            )

    base = ((me - REACH) * blocks).astype(f32)
    win_iota = lax.broadcasted_iota(jnp.int32, (1, PANELS * blocks), 1).astype(f32) + base
    for o in range(offsets):
        place_fwd[o * blocks : (o + 1) * blocks, :] = jnp.where(
            by_sensor[o] == win_iota, 1.0, 0.0
        ).astype(bf16)
    loads[3].wait()
    measured_f32[...] = measured_ref[...].astype(f32).reshape(blocks * frames, width)
    loads[4].wait()

    volumes.pass_on(0)
    for o in range(offsets):
        tile = slice(o * width, (o + 1) * width)
        psf_turned[tile, :] = psf_ref[tile, :].astype(f32).T.astype(bf16)
    volumes.pass_on(1)
    for i, shift in enumerate(SHIFTS):

        @pl.when(inside(-shift))
        def _():
            list_copy(i).wait_recv()

    tables = jnp.concatenate(
        [voxel_win[d, :, :blocks] for d in range(PANELS - 1)]
        + [jnp.full((16, blocks), FAR, f32)],
        axis=1,
    )
    voxel_iota = lax.broadcasted_iota(jnp.int32, (blocks, 1), 0).astype(f32) + (
        me * blocks
    ).astype(f32)
    for o in range(offsets):
        hits = jnp.where(tables[o : o + 1, :] == voxel_iota, 1.0, 0.0)
        place_bwd[o * blocks : (o + 1) * blocks, :] = hits.astype(bf16)
        pairs = jnp.sum(hits, axis=1, keepdims=True)
        ones_rows[:, o * width : (o + 1) * width] = jnp.broadcast_to(pairs, (blocks, width)).astype(
            bf16
        )
    norm[...] = jnp.dot(ones_rows[...], psf_turned[...], preferred_element_type=f32)


    forward(0)
    volumes.pass_on(2)
    forward(1)
    volumes.pass_on(3)
    forward(2)
    ratios.pass_on(0)
    forward(3)
    ratios.pass_on(1)
    backward(0)
    ratios.pass_on(2)
    backward(1)
    ratios.pass_on(3)
    backward(2)
    backward(3)

    for i, shift in enumerate(SHIFTS):

        @pl.when(inside(shift))
        def _():
            list_copy(i).wait_send()

    for j in range(chunks):
        volumes.wait_sent(j)
        ratios.wait_sent(j)


def local(count, volume, measured, background, psf_tiles, pair_sensor, pair_voxel, pair_count):
    blocks, frames, width = volume.shape
    offsets = psf_tiles.shape[0]
    chunks = 4
    lanes = frames // chunks * width
    smem = pl.BlockSpec(memory_space=pltpu.SMEM)
    anywhere = pl.BlockSpec(memory_space=pl.ANY)
    links = len(SHIFTS)
    f32, bf16, dma = jnp.float32, jnp.bfloat16, pltpu.SemaphoreType.DMA
    updated = pl.pallas_call(
        functools.partial(update_kernel, count, chunks),
        out_shape=jax.ShapeDtypeStruct((blocks * frames, width), f32),
        in_specs=[anywhere, anywhere, smem, anywhere, anywhere, anywhere, smem],
        out_specs=pl.BlockSpec(memory_space=pltpu.VMEM),
        scratch_shapes=[
            pltpu.VMEM(volume.shape, bf16),
            pltpu.VMEM(measured.shape, bf16),
            pltpu.VMEM((offsets * width, width), bf16),
            pltpu.VMEM((offsets, 1, blocks), jnp.int32),
            pltpu.VMEM((offsets, 1, blocks), jnp.int32),
            pltpu.VMEM((chunks, PANELS, blocks, lanes), bf16),
            pltpu.VMEM((chunks, PANELS, blocks, lanes), bf16),
            pltpu.VMEM((PANELS - 1, 16, 128), f32),
            pltpu.VMEM((blocks * frames, width), f32),
            pltpu.VMEM((blocks * frames, width), f32),
            pltpu.VMEM((offsets * blocks, PANELS * blocks), bf16),
            pltpu.VMEM((offsets * blocks, PANELS * blocks), bf16),
            pltpu.VMEM((offsets * width, width), bf16),
            pltpu.VMEM((blocks, offsets * width), bf16),
            pltpu.VMEM((blocks, width), f32),
            dma((5,)),
            dma((links,)),
            dma((links,)),
            dma((chunks, OUT_KINDS)),
            dma((chunks, PANELS - 1)),
            dma((chunks, OUT_KINDS)),
            dma((chunks, PANELS - 1)),
        ],
        compiler_params=pltpu.CompilerParams(
            collective_id=0, has_side_effects=True, vmem_limit_bytes=56 * 1024 * 1024
        ),
    )(
        volume,
        measured,
        background.reshape(1, frames),
        psf_tiles.reshape(offsets * width, width),
        pair_sensor.reshape(offsets, 1, blocks),
        pair_voxel.reshape(offsets, 1, blocks),
        pair_count,
    )
    return updated.reshape(blocks, frames, width)


def solution(mesh):
    return jax.shard_map(
        functools.partial(local, mesh.shape["vox"]),
        mesh=mesh,
        in_specs=(
            P("vox", "frm", None),
            P("vox", "frm", None),
            P("frm"),
            P(),
            P("vox", None, None),
            P("vox", None, None),
            P("vox", None),
        ),
        out_specs=P("vox", "frm", None),
        check_vma=False,
    )
```

```python
import functools

import jax
import jax.numpy as jnp
from jax import lax
from jax.experimental import pallas as pl
from jax.experimental.pallas import tpu as pltpu
from jax.sharding import PartitionSpec as P

REACH = 3
PANELS = 2 * REACH + 2
FAR = -1000000.0
SHIFTS = (1, -1, 2, -2, 3, -3)
MESH = pl.DeviceIdType.MESH
OUT_KINDS = 6


def update_kernel(
    count,
    chunks,
    volume_hbm,
    measured_hbm,
    background_ref,
    psf_hbm,
    sensor_hbm,
    voxel_hbm,
    live_ref,
    out_ref,
    volume_ref,
    measured_ref,
    psf_ref,
    sensor_ref,
    voxel_ref,
    volume_win,
    ratio_win,
    voxel_win,
    volume_f32,
    measured_f32,
    place_fwd,
    place_bwd,
    psf_turned,
    ones_rows,
    norm,
    load_sem,
    send_list,
    recv_list,
    send_vol,
    recv_vol,
    send_ratio,
    recv_ratio,
):
    me = lax.axis_index("vox")
    core = lax.rem(me, 2)
    sibling = me + 1 - 2 * core
    blocks, frames, width = volume_ref.shape
    offsets = psf_ref.shape[0] // width
    per = frames // chunks
    lanes = per * width
    f32, bf16 = jnp.float32, jnp.bfloat16

    def inside(shift):
        return (me + shift >= 0) & (me + shift < count)

    loads = [
        pltpu.make_async_copy(source, target, load_sem.at[i])
        for i, (source, target) in enumerate(
            (
                (volume_hbm, volume_ref),
                (sensor_hbm, sensor_ref),
                (voxel_hbm, voxel_ref),
                (measured_hbm, measured_ref),
                (psf_hbm, psf_ref),
            )
        )
    ]
    for load in loads:
        load.start()

    barrier = pltpu.get_barrier_semaphore()
    for shift in SHIFTS:

        @pl.when(inside(shift))
        def _():
            pl.semaphore_signal(barrier, inc=1, device_id={"vox": me + shift}, device_id_type=MESH)

    peers = jnp.minimum(me, REACH) + jnp.minimum(count - 1 - me, REACH)

    loads[0].wait()
    volume_f32[...] = volume_ref[...].astype(f32).reshape(blocks * frames, width)
    for frame in range(frames):
        rows = volume_f32[pl.ds(frame, blocks, stride=frames), :]
        j, k = divmod(frame, per)
        volume_win[j, REACH, :, k * width : (k + 1) * width] = rows.astype(bf16)

    pl.semaphore_wait(barrier, peers)

    class Panels:
        def __init__(self, win, send_sem, recv_sem):
            self.win, self.send_sem, self.recv_sem = win, send_sem, recv_sem

        def copy(self, j, kind, held, target):
            place = REACH + (me + held) - target
            return pltpu.make_async_remote_copy(
                src_ref=self.win.at[j, REACH + held],
                dst_ref=self.win.at[j, place],
                send_sem=self.send_sem.at[j, kind],
                recv_sem=self.recv_sem.at[j, place],
                device_id={"vox": target},
                device_id_type=MESH,
            )

        def wait_panel(self, j, place):
            pltpu.make_async_remote_copy(
                src_ref=self.win.at[j, REACH],
                dst_ref=self.win.at[j, REACH + place],
                send_sem=self.send_sem.at[j, 0],
                recv_sem=self.recv_sem.at[j, REACH + place],
                device_id={"vox": me},
                device_id_type=MESH,
            ).wait_recv()

        def own(self):
            far = me + 6 * core - 3
            direct_up, direct_down = inside(2), inside(-2)
            return (
                (1, 0, me + 2, direct_up),
                (2, 0, me - 2, direct_down),
                (0, 0, far, (far >= 0) & (far < count)),
                (3, 0, sibling, me >= 0),
            )

        def passed(self):
            return ((4, 2, sibling, inside(2)), (5, -2, sibling, inside(-2)))

        def send_own(self, j):
            for kind, held, target, use in self.own():

                @pl.when(use)
                def _():
                    self.copy(j, kind, held, target).start()

        def pass_on(self, j):
            for kind, held, target, use in self.passed():

                @pl.when(use)
                def _():
                    self.wait_panel(j, held)
                    self.copy(j, kind, held, target).start()

        def wait_rest(self, j):
            self.wait_panel(j, 1 - 2 * core)
            far = 6 * core - 3

            @pl.when((me + far >= 0) & (me + far < count))
            def _():
                self.wait_panel(j, far)

            for shift in (2, -2):
                place = 1 - 2 * core + shift

                @pl.when((me + place >= 0) & (me + place < count))
                def _():
                    self.wait_panel(j, place)

        def wait_sent(self, j):
            for kind, held, target, use in (*self.own(), *self.passed()):

                @pl.when(use)
                def _():
                    self.copy(j, kind, held, target).wait_send()

    volumes = Panels(volume_win, send_vol, recv_vol)
    ratios = Panels(ratio_win, send_ratio, recv_ratio)

    def list_copy(i):
        shift = SHIFTS[i]
        return pltpu.make_async_remote_copy(
            src_ref=voxel_win.at[REACH],
            dst_ref=voxel_win.at[REACH - shift],
            send_sem=send_list.at[i],
            recv_sem=recv_list.at[i],
            device_id={"vox": me + shift},
            device_id_type=MESH,
        )

    volumes.send_own(0)

    loads[1].wait()
    loads[2].wait()
    sensor_iota = lax.broadcasted_iota(jnp.int32, (blocks, blocks), 0)
    slot_iota = lax.broadcasted_iota(jnp.int32, (1, blocks), 1)
    lane_iota = lax.broadcasted_iota(jnp.int32, (blocks, 128), 1)
    by_sensor = []
    table = jnp.full((blocks, 128), FAR, f32)
    for o in range(offsets):
        live = slot_iota < live_ref[0, o]
        sensor_row = jnp.where(live, sensor_ref[o], -1)
        voxel_row = voxel_ref[o].astype(f32) - FAR
        column = jnp.sum(
            jnp.where(sensor_row == sensor_iota, voxel_row, 0.0), axis=1, keepdims=True
        ) + FAR
        by_sensor.append(column)
        table = jnp.where(lane_iota == o, column, table)
    turned = table.T
    voxel_win[REACH, :, :blocks] = turned[:8, :]
    voxel_win[REACH, :, blocks:] = turned[8:16, :]

    for i, shift in enumerate(SHIFTS):

        @pl.when(inside(shift))
        def _():
            list_copy(i).start()

    for j in range(1, chunks):
        volumes.send_own(j)

    for j in range(chunks):
        volume_win[j, PANELS - 1] = jnp.zeros((blocks, lanes), bf16)
        ratio_win[j, PANELS - 1] = jnp.zeros((blocks, lanes), bf16)
    for shift in SHIFTS:

        @pl.when(jnp.logical_not(inside(shift)))
        def _():
            for j in range(chunks):
                volume_win[j, REACH + shift] = jnp.zeros((blocks, lanes), bf16)
                ratio_win[j, REACH + shift] = jnp.zeros((blocks, lanes), bf16)
            voxel_win[REACH + shift] = jnp.full((8, 128), FAR, f32)

    def joined(placed):
        return jnp.concatenate(
            [
                jnp.concatenate(
                    [
                        placed[o * blocks : (o + 1) * blocks, k * width : (k + 1) * width]
                        for o in range(offsets)
                    ],
                    axis=1,
                )
                for k in range(per)
            ],
            axis=0,
        )

    def forward(j):
        volumes.wait_rest(j)
        window = volume_win[j].reshape(PANELS * blocks, lanes)
        placed = jnp.dot(place_fwd[...], window, preferred_element_type=f32).astype(bf16)
        projected = jnp.dot(joined(placed), psf_ref[...], preferred_element_type=f32)
        for k in range(per):
            frame = j * per + k
            recorded = measured_f32[pl.ds(frame, blocks, stride=frames), :]
            ratio = recorded / (projected[k * blocks : (k + 1) * blocks] + background_ref[0, frame])
            ratio_win[j, REACH, :, k * width : (k + 1) * width] = ratio.astype(bf16)
        ratios.send_own(j)

    def backward(j):
        ratios.wait_rest(j)
        window = ratio_win[j].reshape(PANELS * blocks, lanes)
        summed = jnp.dot(place_bwd[...], window, preferred_element_type=f32)
        high = summed.astype(bf16)
        low = (summed - high.astype(f32)).astype(bf16)
        back = jnp.dot(joined(high), psf_turned[...], preferred_element_type=f32)
        back = back + jnp.dot(joined(low), psf_turned[...], preferred_element_type=f32)
        for k in range(per):
            frame = j * per + k
            current = volume_f32[pl.ds(frame, blocks, stride=frames), :]
            out_ref[pl.ds(frame, blocks, stride=frames), :] = (
                current * back[k * blocks : (k + 1) * blocks] / norm[...]
            )

    base = ((me - REACH) * blocks).astype(f32)
    win_iota = lax.broadcasted_iota(jnp.int32, (1, PANELS * blocks), 1).astype(f32) + base
    for o in range(offsets):
        place_fwd[o * blocks : (o + 1) * blocks, :] = jnp.where(
            by_sensor[o] == win_iota, 1.0, 0.0
        ).astype(bf16)
    loads[3].wait()
    measured_f32[...] = measured_ref[...].astype(f32).reshape(blocks * frames, width)
    loads[4].wait()

    volumes.pass_on(0)
    for o in range(offsets):
        tile = slice(o * width, (o + 1) * width)
        psf_turned[tile, :] = psf_ref[tile, :].astype(f32).T.astype(bf16)
    volumes.pass_on(1)
    forward(0)
    volumes.pass_on(2)
    for i, shift in enumerate(SHIFTS):

        @pl.when(inside(-shift))
        def _():
            list_copy(i).wait_recv()

    tables = [
        jnp.concatenate(
            [voxel_win[d, :, side * blocks : (side + 1) * blocks] for d in range(PANELS - 1)]
            + [jnp.full((8, blocks), FAR, f32)],
            axis=1,
        )
        for side in range(2)
    ]
    voxel_iota = lax.broadcasted_iota(jnp.int32, (blocks, 1), 0).astype(f32) + (
        me * blocks
    ).astype(f32)
    for o in range(offsets):
        hits = jnp.where(tables[o // 8][o % 8 : o % 8 + 1, :] == voxel_iota, 1.0, 0.0)
        place_bwd[o * blocks : (o + 1) * blocks, :] = hits.astype(bf16)
        pairs = jnp.sum(hits, axis=1, keepdims=True)
        ones_rows[:, o * width : (o + 1) * width] = jnp.broadcast_to(pairs, (blocks, width)).astype(
            bf16
        )
    norm[...] = jnp.dot(ones_rows[...], psf_turned[...], preferred_element_type=f32)


    forward(1)
    volumes.pass_on(3)
    forward(2)
    ratios.pass_on(0)
    forward(3)
    ratios.pass_on(1)
    backward(0)
    ratios.pass_on(2)
    backward(1)
    ratios.pass_on(3)
    backward(2)
    backward(3)

    for i, shift in enumerate(SHIFTS):

        @pl.when(inside(shift))
        def _():
            list_copy(i).wait_send()

    for j in range(chunks):
        volumes.wait_sent(j)
        ratios.wait_sent(j)


def local(count, volume, measured, background, psf_tiles, pair_sensor, pair_voxel, pair_count):
    blocks, frames, width = volume.shape
    offsets = psf_tiles.shape[0]
    chunks = 4
    lanes = frames // chunks * width
    smem = pl.BlockSpec(memory_space=pltpu.SMEM)
    anywhere = pl.BlockSpec(memory_space=pl.ANY)
    links = len(SHIFTS)
    f32, bf16, dma = jnp.float32, jnp.bfloat16, pltpu.SemaphoreType.DMA
    updated = pl.pallas_call(
        functools.partial(update_kernel, count, chunks),
        out_shape=jax.ShapeDtypeStruct((blocks * frames, width), f32),
        in_specs=[anywhere, anywhere, smem, anywhere, anywhere, anywhere, smem],
        out_specs=pl.BlockSpec(memory_space=pltpu.VMEM),
        scratch_shapes=[
            pltpu.VMEM(volume.shape, bf16),
            pltpu.VMEM(measured.shape, bf16),
            pltpu.VMEM((offsets * width, width), bf16),
            pltpu.VMEM((offsets, 1, blocks), jnp.int32),
            pltpu.VMEM((offsets, 1, blocks), jnp.int32),
            pltpu.VMEM((chunks, PANELS, blocks, lanes), bf16),
            pltpu.VMEM((chunks, PANELS, blocks, lanes), bf16),
            pltpu.VMEM((PANELS - 1, 8, 128), f32),
            pltpu.VMEM((blocks * frames, width), f32),
            pltpu.VMEM((blocks * frames, width), f32),
            pltpu.VMEM((offsets * blocks, PANELS * blocks), bf16),
            pltpu.VMEM((offsets * blocks, PANELS * blocks), bf16),
            pltpu.VMEM((offsets * width, width), bf16),
            pltpu.VMEM((blocks, offsets * width), bf16),
            pltpu.VMEM((blocks, width), f32),
            dma((5,)),
            dma((links,)),
            dma((links,)),
            dma((chunks, OUT_KINDS)),
            dma((chunks, PANELS - 1)),
            dma((chunks, OUT_KINDS)),
            dma((chunks, PANELS - 1)),
        ],
        compiler_params=pltpu.CompilerParams(
            collective_id=0, has_side_effects=True, vmem_limit_bytes=56 * 1024 * 1024
        ),
    )(
        volume,
        measured,
        background.reshape(1, frames),
        psf_tiles.reshape(offsets * width, width),
        pair_sensor.reshape(offsets, 1, blocks),
        pair_voxel.reshape(offsets, 1, blocks),
        pair_count,
    )
    return updated.reshape(blocks, frames, width)


def solution(mesh):
    return jax.shard_map(
        functools.partial(local, mesh.shape["vox"]),
        mesh=mesh,
        in_specs=(
            P("vox", "frm", None),
            P("vox", "frm", None),
            P("frm"),
            P(),
            P("vox", None, None),
            P("vox", None, None),
            P("vox", None),
        ),
        out_specs=P("vox", "frm", None),
        check_vma=False,
    )
```
